32 devices in a mesh: chan: 4 (over y, core), tile: 8 (over z, x).
Axes of the slice: x: 2, y: 2, z: 4, core: 2. Of those that a mesh axis runs over, the one named last changes fastest.
Arguments:
- intensity: bfloat16 [256, 256, 512], P('chan', 'tile'), may hold values from -12 to 12
- block_pick: int32 [8, 4, 4], P('tile', 'chan'), may hold values from 0 to 7, as said below
- owner_tile: int32 [8, 4, 4], P('tile', 'chan'), may hold values from 0 to 7, as said below
- source_index: int32 [8, 4, 4], P('tile', 'chan'), may hold values from 0 to 15
- mask_low: int32 [8, 4, 4, 1024], P('tile', 'chan'), may hold values from 0 to 63
- mask_high: int32 [8, 4, 4, 1024], P('tile', 'chan'), may hold values from 64 to 128
Outputs:
- moment_maps: float32 [8, 4, 8, 2, 1024], P('tile', 'chan')
- spectra: float32 [8, 4, 16, 256], P('tile', 'chan')
- smoothed: bfloat16 [256, 256, 512], P(None, 'tile', 'chan')
The draws below stay inside these ranges and needn't reach their ends.
Inputs may be any that keep to these rules, and one draw needn't show every extreme that they name: `block_pick`: the 4 block numbers of one device are distinct. `owner_tile`: among the 4 sends of one device no owner appears more than 2 times; in every chan index some owner receives exactly 2 blocks from every device of that chan index.
All inputs are finite; a program needn't handle non-finite values.
Results may differ from the reference program's by a relative error of at most 0.0021.
Values may be sent and summed in bfloat16 or wider, within the bound.
A program may use at most 128 MiB of HBM per device.

```python
import jax
import jax.numpy as jnp
from jax import lax

TY = 32
TX = 128
BCH = 128
BPIX = 32
RADIUS = 2
CAP = 2
SRC_DEV = 16
NCH = 256
NY = 256
NX = 512
BLK_DEV = 8
SEND = 4
N_CHAN = 4
N_TILE = 8


def draw_block_pick(key, part):
    device_ids = jnp.arange(N_TILE * N_CHAN, dtype=jnp.int32)

    def per_device(device_id):
        return jax.random.permutation(jax.random.fold_in(key, device_id + 7), BLK_DEV)[:SEND]
    picked = jax.vmap(per_device)(device_ids)
    return picked.reshape(N_TILE, N_CHAN, SEND).astype(jnp.int32)


def draw_owner_tile(key, part):
    hot_tiles = jax.random.randint(jax.random.fold_in(key, 11), (N_CHAN,), 0, N_TILE)
    remaining = SEND - CAP
    fewest = max(0, remaining - (N_TILE - 1))
    device_ids = jnp.arange(N_TILE * N_CHAN, dtype=jnp.int32)

    def per_device(device_id, hot_tile):
        device_key = jax.random.fold_in(key, device_id + 100)
        subkeys = jax.random.split(device_key, 3)
        doubles = jax.random.randint(subkeys[0], (), fewest, remaining // 2 + 1)
        others = jax.random.permutation(subkeys[1], N_TILE - 1).astype(jnp.int32)
        others = others + (others >= hot_tile).astype(jnp.int32)
        position = jnp.arange(SEND, dtype=jnp.int32)
        offset_pos = position - CAP
        double_pick = others[jnp.clip(offset_pos // 2, 0, N_TILE - 2)]
        single_pick = others[jnp.clip(offset_pos - doubles, 0, N_TILE - 2)]
        chosen = jnp.where(position < CAP, hot_tile, jnp.where(offset_pos < 2 * doubles, double_pick, single_pick))
        return chosen[jax.random.permutation(subkeys[2], SEND)]
    result = jax.vmap(per_device)(device_ids, hot_tiles[device_ids % N_CHAN])
    return result.reshape(N_TILE, N_CHAN, SEND).astype(jnp.int32)


def with_ends(values, rng, low, top_value):
    place = [jax.random.randint(jax.random.fold_in(rng, axis), (), 0, length) for axis, length in enumerate(values.shape)]
    longest = values.shape.index(max(values.shape))
    beside = place[:longest] + [(place[longest] + 1) % values.shape[longest]] + place[longest + 1:]
    return values.at[tuple(place)].set(low).at[tuple(beside)].set(top_value)


def levels(key, extent, shards, low, top_value):
    factor_of = 1.0
    for dim, blocks in shards:
        steps = jax.random.uniform(jax.random.fold_in(jax.random.fold_in(key, 6), dim), (blocks,), jnp.float32, low / len(shards), top_value / len(shards))
        factor_of = factor_of * jnp.repeat(jnp.exp(steps), extent[dim] // blocks).reshape((-1,) + (1,) * (len(extent) - 1 - dim))
    return factor_of


def normal_values(own_key, shape, deviation, most, pieces=(), kind=jnp.bfloat16):
    values = deviation * jax.random.normal(own_key, shape, jnp.float32)
    if pieces:
        values = values * levels(own_key, shape, pieces, -0.22, 0.18)
    return jnp.clip(values, -most, most).astype(kind)


def setup_inputs(seed: int = 0) -> dict:
    key_list = jax.random.split(jax.random.key(seed), 7)
    intensity = normal_values(key_list[0], (NCH, NY, NX), 2.0, 12.0, ((0, 4), (1, 8)))
    block_pick = draw_block_pick(jax.random.fold_in(key_list[6], 71), 0)
    owner_tile = draw_owner_tile(jax.random.fold_in(key_list[6], 71), 0)
    source_index = with_ends(jax.random.randint(key_list[3], (N_TILE, N_CHAN, SEND), 0, SRC_DEV), jax.random.fold_in(key_list[3], 1), 0, SRC_DEV - 1).astype(jnp.int32)
    mask_low = with_ends(jax.random.randint(key_list[4], (N_TILE, N_CHAN, SEND, BPIX * BPIX), 0, BCH // 2), jax.random.fold_in(key_list[4], 1), 0, (BCH // 2) - 1).astype(jnp.int32)
    mask_high = with_ends(jax.random.randint(key_list[5], (N_TILE, N_CHAN, SEND, BPIX * BPIX), BCH // 2, BCH + 1), jax.random.fold_in(key_list[5], 1), BCH // 2, BCH).astype(jnp.int32)
    return dict(intensity=intensity, block_pick=block_pick, owner_tile=owner_tile, source_index=source_index, mask_low=mask_low, mask_high=mask_high)


SIGMA = 1.5


def gauss_weights():
    offsets = jnp.arange(-RADIUS, RADIUS + 1).astype(jnp.float32)
    raw_weights = jnp.exp(-offsets * offsets / (2.0 * SIGMA * SIGMA))
    return raw_weights / jnp.sum(raw_weights)


def reference(intensity, block_pick, owner_tile, source_index, mask_low, mask_high):
    chan_total, rows_total, cols_total = intensity.shape
    weights = gauss_weights()

    def smooth_plane(chan_index):
        middle = lax.dynamic_index_in_dim(intensity, chan_index, 0, keepdims=False).astype(jnp.float32)
        before = lax.dynamic_index_in_dim(intensity, jnp.maximum(chan_index - 1, 0), 0, keepdims=False).astype(jnp.float32)
        before = before * (chan_index > 0).astype(jnp.float32)
        after = lax.dynamic_index_in_dim(intensity, jnp.minimum(chan_index + 1, chan_total - 1), 0, keepdims=False).astype(jnp.float32)
        after = after * (chan_index < chan_total - 1).astype(jnp.float32)
        hanning = 0.5 * middle + 0.25 * (before + after)
        padded = jnp.pad(hanning, RADIUS)
        row_pass = sum(weights[offset] * padded[offset:offset + rows_total, :] for offset in range(2 * RADIUS + 1))
        col_pass = sum(weights[offset] * row_pass[:, offset:offset + cols_total] for offset in range(2 * RADIUS + 1))
        return col_pass.astype(jnp.bfloat16)

    smoothed = lax.map(smooth_plane, jnp.arange(chan_total, dtype=jnp.int32))

    tile_count, chan_count, send_count = block_pick.shape
    block_rows = TY // BPIX
    block_cols = TX // BPIX
    chan_blocks = chan_total // BCH
    pixel_count = BPIX * BPIX
    tile_ids = jnp.broadcast_to(jnp.arange(tile_count, dtype=jnp.int32)[:, None, None], block_pick.shape)
    chan_ids = jnp.broadcast_to(jnp.arange(chan_count, dtype=jnp.int32)[None, :, None], block_pick.shape)
    chan_block = block_pick // (block_rows * block_cols)
    within = block_pick % (block_rows * block_cols)
    row_start = tile_ids * TY + (within // block_cols) * BPIX
    col_start = chan_ids * TX + (within % block_cols) * BPIX

    def measure_one(packed):
        block_chan, row_first, col_first, low_row, high_row = packed
        block = lax.dynamic_slice(smoothed, (block_chan * BCH, row_first, col_first), (BCH, BPIX, BPIX))
        block = block.astype(jnp.float32).reshape(BCH, pixel_count)
        chan_pos = jnp.arange(BCH, dtype=jnp.int32)[:, None]
        inside = (low_row[None, :] <= chan_pos) & (chan_pos < high_row[None, :])
        masked = jnp.where(inside, block, 0.0)
        return jnp.sum(masked, axis=0), jnp.sum(masked, axis=1)

    maps_flat, spectra_flat = lax.map(measure_one, (chan_block.reshape(-1), row_start.reshape(-1), col_start.reshape(-1), mask_low.reshape(-1, pixel_count), mask_high.reshape(-1, pixel_count)))

    positions = jnp.arange(send_count, dtype=jnp.int32)
    earlier = positions[None, :] < positions[:, None]
    same_owner = owner_tile[..., None, :] == owner_tile[..., :, None]
    ranking = jnp.sum((same_owner & earlier).astype(jnp.int32), axis=-1).astype(jnp.int32)

    moment_maps = jnp.zeros((tile_count, chan_count, tile_count, CAP, pixel_count), jnp.float32)
    moment_maps = moment_maps.at[owner_tile.reshape(-1), chan_ids.reshape(-1), tile_ids.reshape(-1), ranking.reshape(-1)].set(maps_flat)
    spectra = jnp.zeros((tile_count, chan_count, SRC_DEV, chan_blocks, BCH), jnp.float32)
    spectra = spectra.at[owner_tile.reshape(-1), chan_ids.reshape(-1), source_index.reshape(-1), chan_block.reshape(-1)].add(spectra_flat)
    return moment_maps, spectra.reshape(tile_count, chan_count, SRC_DEV, chan_blocks * BCH), smoothed
```

```python
import functools

import jax
import jax.numpy as jnp
import numpy as np
from jax import lax
from jax.experimental import pallas as pl
from jax.experimental.pallas import tpu as pltpu
from jax.sharding import PartitionSpec as P

BCH = 128
BPIX = 32
CAP = 2
SRC_DEV = 16
SIGMA = 1.5
KC = 8
MESH = pl.DeviceIdType.MESH
F32 = jnp.float32
BF16 = jnp.bfloat16


def gauss_taps():
    off = np.arange(-2, 3).astype(np.float32)
    raw = np.exp(-off * off / np.float32(2.0 * SIGMA * SIGMA))
    g = (raw / raw.sum()).astype(np.float32)
    return [float(g[2]), float(g[3]), float(g[4])]


def split_taps(taps):
    hi = [float(np.float32(np.asarray(v, dtype=jnp.bfloat16))) for v in taps]
    lo = [v - h for v, h in zip(taps, hi)]
    return hi, lo


def banded(dist, same, taps):
    value = jnp.where(dist == 0, taps[0], jnp.where(dist == 1, taps[1], jnp.where(dist == 2, taps[2], 0.0)))
    return jnp.where(same, value, 0.0).astype(BF16)


def iota(shape, dim):
    return lax.broadcasted_iota(jnp.int32, shape, dim)


def kernel(
    n_chan, n_tile, send_count,
    x_ref, pick_ref, owner_ref, source_ref, low_ref, high_ref,
    maps_ref, spec_ref, out_ref,
    amat, bmat, up_out, dn_out, top_in, bot_in, zs, stage, tile_low, tile_high, rep,
    moments, colsum, msg, rcv,
    halo_send, halo_recv, edge_send, edge_recv, data_send, data_recv, own_send, own_recv,
):
    t = lax.axis_index("tile")
    c = lax.axis_index("chan")
    nch, rows, cols = x_ref.shape
    nk = nch // KC
    nq = n_chan * nch // BCH
    ny = n_chan // 2
    taps = gauss_taps()
    hi, lo = split_taps(taps)
    yy, core = c // 2, c % 2
    peers = []
    for dy in range(1, ny):
        for dc in range(2):
            peers.append(lax.rem(yy + dy, ny) * 2 + lax.rem(core + dc, 2))
    peers.append(yy * 2 + 1 - core)
    tiles = [lax.rem(t + d, n_tile) for d in range(1, n_tile)]

    barrier = pltpu.get_barrier_semaphore()
    for p in peers:
        pl.semaphore_signal(barrier, inc=1, device_id=(p, t), device_id_type=MESH)
    for p in tiles:
        pl.semaphore_signal(barrier, inc=1, device_id=(c, p), device_id_type=MESH)

    m = KC * rows

    def chunk_at(p):
        return jnp.where(p == 0, 0, jnp.where(p == 1, nk - 1, p - 1))

    srow, scol = iota((32, m), 0), iota((32, m), 1)
    within = lax.rem(srow, 16)
    wanted = lax.div(within, 2) * rows + lax.rem(within, 2) + jnp.where(srow >= 16, rows - 2, 0)
    select = jnp.where(scol == wanted, 1.0, 0.0).astype(BF16)

    def pack(p, carry):
        k = chunk_at(p)
        x = x_ref[pl.ds(k * KC, KC)].reshape(m, cols)
        picked = jnp.dot(select, x, preferred_element_type=F32).astype(BF16)
        up_out[pl.ds(pl.multiple_of(p * 16, 16), 16), :] = picked[:16]
        dn_out[pl.ds(pl.multiple_of(p * 16, 16), 16), :] = picked[16:]
        return carry

    lax.fori_loop(0, nk, pack, 0)

    arow, acol = iota((m, m), 0), iota((m, m), 1)
    same = lax.div(arow, rows) == lax.div(acol, rows)
    amat[0] = banded(jnp.abs(arow - acol), same, hi)
    amat[1] = banded(jnp.abs(arow - acol), same, lo)
    brow, bcol = iota((m, 64), 0), iota((m, 64), 1)
    inner = lax.rem(bcol, 16)
    place = lax.rem(inner, 2) + jnp.where(lax.rem(bcol, 32) >= 16, rows, -2)
    same = lax.div(inner, 2) == lax.div(brow, rows)
    dist = jnp.abs(lax.rem(brow, rows) - place)
    bmat[...] = jnp.where(bcol < 32, banded(dist, same, hi).astype(F32), banded(dist, same, lo).astype(F32)).astype(BF16)

    @pl.when(t == 0)
    def _():
        top_in[...] = jnp.zeros_like(top_in)

    @pl.when(t == n_tile - 1)
    def _():
        bot_in[...] = jnp.zeros_like(bot_in)

    @pl.when(c == 0)
    def _():
        zs[0] = jnp.zeros((rows, cols), F32)

    @pl.when(c == n_chan - 1)
    def _():
        zs[nch + 1] = jnp.zeros((rows, cols), F32)

    pl.semaphore_wait(barrier, len(peers) + len(tiles))

    def halo(direction, i):
        part = pl.ds(i * 32, 32)
        src, dst = (up_out, bot_in) if direction == 0 else (dn_out, top_in)
        target = lax.max(t - 1, 0) if direction == 0 else lax.min(t + 1, n_tile - 1)
        return pltpu.make_async_remote_copy(
            src_ref=src.at[part, :], dst_ref=dst.at[part, :],
            send_sem=halo_send.at[direction, i], recv_sem=halo_recv.at[direction, i],
            device_id=(c, target), device_id_type=MESH,
        )

    nm = nk // 2
    for i in range(nm):
        @pl.when(t > 0)
        def _():
            halo(0, i).start()

        @pl.when(t < n_tile - 1)
        def _():
            halo(1, i).start()

    def wait_halo(i):
        @pl.when(t < n_tile - 1)
        def _():
            halo(0, i).wait_recv()

        @pl.when(t > 0)
        def _():
            halo(1, i).wait_recv()

    def row_pass(p, carry):
        k = chunk_at(p)
        x = x_ref[pl.ds(k * KC, KC)].reshape(m, cols)
        part = pl.ds(pl.multiple_of(p * 16, 16), 16)
        rim = jnp.concatenate([top_in[part, :], bot_in[part, :]] * 2, axis=0)
        z = jnp.dot(amat[0], x, preferred_element_type=F32)
        z += jnp.dot(amat[1], x, preferred_element_type=F32)
        z += jnp.dot(bmat[...], rim, preferred_element_type=F32)
        zs[pl.ds(k * KC + 1, KC)] = z.reshape(KC, rows, cols)
        return carry

    def edge(direction):
        src, dst = (1, nch + 1) if direction == 0 else (nch, 0)
        target = lax.max(c - 1, 0) if direction == 0 else lax.min(c + 1, n_chan - 1)
        return pltpu.make_async_remote_copy(
            src_ref=zs.at[src], dst_ref=zs.at[dst],
            send_sem=edge_send.at[direction], recv_sem=edge_recv.at[direction],
            device_id=(target, t), device_id_type=MESH,
        )

    def data(slot, source, target, k):
        return pltpu.make_async_remote_copy(
            src_ref=stage.at[target, pl.ds(k * KC, KC)],
            dst_ref=out_ref.at[pl.ds(source * nch + k * KC, KC)],
            send_sem=data_send.at[slot, k], recv_sem=data_recv.at[source, k],
            device_id=(target, t), device_id_type=MESH,
        )

    lane = iota((rows, cols), 1)

    def finish(k, carry):
        def one(i, carry):
            ch = k * KC + i
            h = 0.5 * zs[ch + 1] + 0.25 * (zs[ch] + zs[ch + 2])
            near = jnp.where(lane >= 1, pltpu.roll(h, 1, 1), 0.0) + jnp.where(
                lane < cols - 1, pltpu.roll(h, cols - 1, 1), 0.0
            )
            far = jnp.where(lane >= 2, pltpu.roll(h, 2, 1), 0.0) + jnp.where(
                lane < cols - 2, pltpu.roll(h, cols - 2, 1), 0.0
            )
            res = (taps[0] * h + taps[1] * near + taps[2] * far).astype(BF16)
            width = cols // n_chan
            for j in range(n_chan):
                stage[j, ch] = res[:, j * width : (j + 1) * width]
            return carry

        lax.fori_loop(0, KC, one, 0, unroll=2)
        for slot, p in enumerate(peers):
            data(slot, c, p, k).start()
        out_ref[pl.ds(c * nch + k * KC, KC)] = stage[c, pl.ds(k * KC, KC)]
        return carry

    wait_halo(0)
    lax.fori_loop(0, 2, row_pass, 0)

    @pl.when(c > 0)
    def _():
        edge(0).start()

    @pl.when(c < n_chan - 1)
    def _():
        edge(1).start()

    for i in range(1, nm):
        wait_halo(i)
        lax.fori_loop(2 * i, 2 * i + 2, row_pass, 0)
        lax.fori_loop(max(1, 2 * i - 2), 2 * i if i < nm - 1 else 2 * i + 1, finish, 0)

    @pl.when(c < n_chan - 1)
    def _():
        edge(0).wait_recv()

    @pl.when(c > 0)
    def _():
        edge(1).wait_recv()

    lax.fori_loop(0, 2, lambda i, carry: finish(i * (nk - 1), carry), 0)

    width = cols // n_chan
    per = width // BPIX
    r, l = iota((rows, width), 0), iota((rows, width), 1)
    group = lax.div(l, BPIX)
    turn = lax.rem(group - lax.rem(r, per) + per, per)
    for q in range(nq):
        tile_low[q] = jnp.zeros((rows, width), jnp.int32)
        tile_high[q] = jnp.zeros((rows, width), jnp.int32)
    picks = [pick_ref[0, 0, s] for s in range(send_count)]
    owners = [owner_ref[0, 0, s] for s in range(send_count)]
    sources = [source_ref[0, 0, s] for s in range(send_count)]
    slots = []
    for s in range(send_count):
        rank = jnp.int32(0)
        for e in range(s):
            rank = rank + jnp.where(owners[e] == owners[s], 1, 0)
        slots.append(owners[s] * CAP + rank)
    qs = [lax.div(p, per) for p in picks]
    vs = [lax.rem(p, per) for p in picks]
    for s in range(send_count):
        for ends_ref, grid in ((low_ref, tile_low), (high_ref, tile_high)):
            for a in range(rows // per):
                line = ends_ref[0, 0, pl.ds(s, 1), pl.ds(a * width, width)]
                rep[pl.ds(a * per, per), :] = jnp.broadcast_to(line, (per, width))
            base = rep[...]
            value = base
            for i in range(1, per):
                value = jnp.where(turn == i, pltpu.roll(base, i * BPIX, 1), value)
            for q in range(nq):
                hit = (group == vs[s]) & (qs[s] == q)
                grid[q] = jnp.where(hit, value, grid[q])

    moments[...] = jnp.zeros_like(moments)
    chans = iota((KC, rows, width), 0)

    def measure(source, k):
        base = pl.multiple_of(source * nch + k * KC, KC)
        q = lax.div(base, BCH)
        v = out_ref[pl.ds(base, KC)].astype(F32)
        pos = chans + lax.rem(base, BCH)
        inside = (tile_low[q][None] <= pos) & (pos < tile_high[q][None])
        v = jnp.where(inside, v, 0.0)
        moments[q] += jnp.sum(v, axis=0)
        colsum[pl.ds(base, KC), :] = jnp.sum(v, axis=1)

    def order(i):
        return jnp.where(i < nk - 2, i + 1, jnp.where(i == nk - 2, 0, nk - 1))

    def own(k, carry):
        measure(c, k)
        return carry

    lax.fori_loop(0, nk, own, 0)

    def arrive_same(i, carry):
        k = order(i)
        data(len(peers) - 1, peers[-1], c, k).wait_recv()
        measure(peers[-1], k)
        return carry

    lax.fori_loop(0, nk, arrive_same, 0)

    def arrive(i, carry):
        k = order(i)
        for slot, p in enumerate(peers[:-1]):
            data(slot, p, c, k).wait_recv()
            measure(p, k)
        return carry

    lax.fori_loop(0, nk, arrive, 0)

    fold = jnp.where(lax.div(iota((rows // per, rows), 1), per) == iota((rows // per, rows), 0), 1.0, 0.0)
    maps = []
    for s in range(send_count):
        total = jnp.zeros((rows, width), F32)
        for q in range(nq):
            total = jnp.where((group == vs[s]) & (qs[s] == q), moments[q], total)
        step = BPIX
        while step < width:
            total = total + pltpu.roll(total, step, 1)
            step *= 2
        total = jnp.where(group == lax.rem(r, per), total, 0.0)
        maps.append(jnp.dot(fold, total, precision=lax.Precision.HIGHEST, preferred_element_type=F32))
    entries = n_tile * CAP
    er, el = iota((entries, width), 0), iota((entries, width), 1)
    eg = lax.div(el, BPIX)
    spectra = jnp.zeros((entries, BCH), F32)
    tags = jnp.zeros((entries, width), F32)
    for q in range(nq):
        chosen = jnp.zeros((entries, width), F32)
        for s in range(send_count):
            chosen = jnp.where((er == slots[s]) & (eg == vs[s]) & (qs[s] == q), 1.0, chosen)
        spectra += lax.dot_general(
            chosen, colsum[pl.ds(q * BCH, BCH), :], (((1,), (1,)), ((), ())),
            precision=lax.Precision.HIGHEST, preferred_element_type=F32,
        )
    for s in range(send_count):
        tags = jnp.where(er == slots[s], (sources[s] * nq + qs[s]).astype(F32), tags)
    for o in range(n_tile):
        for n in range(CAP):
            total = jnp.zeros((rows // per, width), F32)
            for s in range(send_count):
                total = jnp.where(slots[s] == o * CAP + n, maps[s], total)
            msg[o, pl.ds(n * 8, 8), :] = total
        part = slice(o * CAP, o * CAP + CAP)
        msg[o, pl.ds(16, 8), :] = jnp.concatenate(
            [spectra[part], tags[part], jnp.zeros((4, width), F32)], axis=0
        )

    def to_owner(d, source, target):
        return pltpu.make_async_remote_copy(
            src_ref=msg.at[target], dst_ref=rcv.at[source],
            send_sem=own_send.at[d], recv_sem=own_recv.at[source],
            device_id=(c, target), device_id_type=MESH,
        )

    for d, p in enumerate(tiles):
        to_owner(d, t, p).start()
    rcv[t] = msg[t]

    for i in range(nm):
        @pl.when(t > 0)
        def _():
            halo(0, i).wait_send()

        @pl.when(t < n_tile - 1)
        def _():
            halo(1, i).wait_send()

    @pl.when(c > 0)
    def _():
        edge(0).wait_send()

    @pl.when(c < n_chan - 1)
    def _():
        edge(1).wait_send()

    def left(k, carry):
        for slot, p in enumerate(peers):
            data(slot, c, p, k).wait_send()
        return carry

    lax.fori_loop(0, nk, left, 0)
    for d, p in enumerate(tiles):
        to_owner(d, t, p).wait_send()
    for d, p in enumerate(tiles):
        to_owner(d, p, p).wait_recv()

    maps_ref[...] = rcv[:, :16, :]
    which = iota((SRC_DEV, width), 0) * nq
    totals = [jnp.zeros((SRC_DEV, BCH), F32) for _ in range(nq)]
    for i in range(n_tile):
        for n in range(CAP):
            line = rcv[i, pl.ds(16 + n, 1), :]
            tag = rcv[i, pl.ds(18 + n, 1), :]
            for q in range(nq):
                totals[q] = totals[q] + jnp.where(tag == (which + q).astype(F32), line, 0.0)
    for q in range(nq):
        spec_ref[:, pl.ds(q * BCH, BCH)] = totals[q]


def solution(mesh):
    n_chan, n_tile = mesh.shape["chan"], mesh.shape["tile"]

    def step(intensity, block_pick, owner_tile, source_index, mask_low, mask_high):
        nch, rows, cols = intensity.shape
        width = cols // n_chan
        send_count = block_pick.shape[-1]
        total = nch * n_chan
        nq = total // BCH
        nk = nch // KC
        vmem = pl.BlockSpec(memory_space=pltpu.VMEM)
        smem = pl.BlockSpec(memory_space=pltpu.SMEM)
        dma = pltpu.SemaphoreType.DMA
        maps, spectra, smoothed = pl.pallas_call(
            functools.partial(kernel, n_chan, n_tile, send_count),
            out_shape=(
                jax.ShapeDtypeStruct((n_tile, CAP * 8, 128), F32),
                jax.ShapeDtypeStruct((SRC_DEV, total), F32),
                jax.ShapeDtypeStruct((total, rows, width), BF16),
            ),
            in_specs=[vmem, smem, smem, smem, vmem, vmem],
            out_specs=(vmem, vmem, vmem),
            scratch_shapes=[
                pltpu.VMEM((2, KC * rows, KC * rows), BF16),
                pltpu.VMEM((KC * rows, 64), BF16),
                pltpu.VMEM((nch * 2, cols), BF16),
                pltpu.VMEM((nch * 2, cols), BF16),
                pltpu.VMEM((nch * 2, cols), BF16),
                pltpu.VMEM((nch * 2, cols), BF16),
                pltpu.VMEM((nch + 2, rows, cols), F32),
                pltpu.VMEM((n_chan, nch, rows, width), BF16),
                pltpu.VMEM((nq, rows, width), jnp.int32),
                pltpu.VMEM((nq, rows, width), jnp.int32),
                pltpu.VMEM((rows, width), jnp.int32),
                pltpu.VMEM((nq, rows, width), F32),
                pltpu.VMEM((total, width), F32),
                pltpu.VMEM((n_tile, 24, width), F32),
                pltpu.VMEM((n_tile, 24, width), F32),
                dma((2, nk // 2)), dma((2, nk // 2)), dma((2,)), dma((2,)),
                dma((n_chan - 1, nk)), dma((n_chan, nk)),
                dma((n_tile - 1,)), dma((n_tile,)),
            ],
            compiler_params=pltpu.CompilerParams(
                collective_id=0, has_side_effects=True, vmem_limit_bytes=48 * 1024 * 1024
            ),
        )(intensity, block_pick, owner_tile, source_index, mask_low, mask_high)
        return (
            maps.reshape(1, 1, n_tile, CAP, 8 * 128),
            spectra.reshape(1, 1, SRC_DEV, total),
            smoothed,
        )

    return jax.shard_map(
        step,
        mesh=mesh,
        in_specs=(
            P("chan", "tile", None),
            P("tile", "chan", None),
            P("tile", "chan", None),
            P("tile", "chan", None),
            P("tile", "chan", None, None),
            P("tile", "chan", None, None),
        ),
        out_specs=(
            P("tile", "chan", None, None, None),
            P("tile", "chan", None, None),
            P(None, "tile", "chan"),
        ),
        check_vma=False,
    )
```

```python
import functools

import jax
import jax.numpy as jnp
import numpy as np
from jax import lax
from jax.experimental import pallas as pl
from jax.experimental.pallas import tpu as pltpu
from jax.sharding import PartitionSpec as P

BCH = 128
BPIX = 32
CAP = 2
SRC_DEV = 16
SIGMA = 1.5
KC = 8
MESH = pl.DeviceIdType.MESH
F32 = jnp.float32
BF16 = jnp.bfloat16


def gauss_taps():
    off = np.arange(-2, 3).astype(np.float32)
    raw = np.exp(-off * off / np.float32(2.0 * SIGMA * SIGMA))
    g = (raw / raw.sum()).astype(np.float32)
    return [float(g[2]), float(g[3]), float(g[4])]


def split_taps(taps):
    hi = [float(np.float32(np.asarray(v, dtype=jnp.bfloat16))) for v in taps]
    lo = [v - h for v, h in zip(taps, hi)]
    return hi, lo


def banded(dist, same, taps):
    value = jnp.where(dist == 0, taps[0], jnp.where(dist == 1, taps[1], jnp.where(dist == 2, taps[2], 0.0)))
    return jnp.where(same, value, 0.0).astype(BF16)


def iota(shape, dim):
    return lax.broadcasted_iota(jnp.int32, shape, dim)


def kernel(
    n_chan, n_tile, send_count,
    x_hbm, pick_hbm, owner_hbm, source_hbm, low_hbm, high_hbm,
    maps_ref, spec_ref, out_ref,
    x_ref, pick_ref, owner_ref, source_ref, low_ref, high_ref,
    amat, bmat, up_out, dn_out, top_in, bot_in, zs, stage, tile_low, tile_high, rep,
    moments, colsum, msg, rcv, pick_mat,
    x_sem, arg_sem, halo_send, halo_recv, edge_send, edge_recv, data_send, data_recv, own_send, own_recv,
):
    t = lax.axis_index("tile")
    c = lax.axis_index("chan")
    nch, rows, cols = x_ref.shape
    nk = nch // KC
    nq = n_chan * nch // BCH
    ny = n_chan // 2
    taps = gauss_taps()
    hi, lo = split_taps(taps)
    yy, core = c // 2, c % 2
    peers = []
    for dy in range(1, ny):
        for dc in range(2):
            peers.append(lax.rem(yy + dy, ny) * 2 + lax.rem(core + dc, 2))
    peers.append(yy * 2 + 1 - core)
    tiles = [lax.rem(t + d, n_tile) for d in range(1, n_tile)]

    def fetch(p):
        part = pl.ds(p * KC, KC)
        return pltpu.make_async_copy(x_hbm.at[part], x_ref.at[part], x_sem.at[p])

    small = [
        pltpu.make_async_copy(src, dst, arg_sem.at[i])
        for i, (src, dst) in enumerate((
            (pick_hbm, pick_ref), (owner_hbm, owner_ref), (source_hbm, source_ref),
            (low_hbm, low_ref), (high_hbm, high_ref),
        ))
    ]
    barrier = pltpu.get_barrier_semaphore()
    for p in peers:
        pl.semaphore_signal(barrier, inc=1, device_id=(p, t), device_id_type=MESH)
    for p in tiles:
        pl.semaphore_signal(barrier, inc=1, device_id=(c, p), device_id_type=MESH)

    for p in range(nk):
        fetch(p).start()
    for copy in small:
        copy.start()
    m = KC * rows

    srow, scol = iota((32, m), 0), iota((32, m), 1)
    within = lax.rem(srow, 16)
    wanted = lax.div(within, 2) * rows + lax.rem(within, 2) + jnp.where(srow >= 16, rows - 2, 0)
    select = jnp.where(scol == wanted, 1.0, 0.0).astype(BF16)

    def pack(k):
        fetch(k).wait()
        x = x_ref[pl.ds(k * KC, KC)].reshape(m, cols)
        picked = jnp.dot(select, x, preferred_element_type=F32).astype(BF16)
        up_out[pl.ds(pl.multiple_of(k * 16, 16), 16), :] = picked[:16]
        dn_out[pl.ds(pl.multiple_of(k * 16, 16), 16), :] = picked[16:]

    pack(0)
    pl.semaphore_wait(barrier, len(peers) + len(tiles))

    def halo(direction, i):
        part = pl.ds(i * 16, 16)
        src, dst = (up_out, bot_in) if direction == 0 else (dn_out, top_in)
        target = lax.max(t - 1, 0) if direction == 0 else lax.min(t + 1, n_tile - 1)
        return pltpu.make_async_remote_copy(
            src_ref=src.at[part, :], dst_ref=dst.at[part, :],
            send_sem=halo_send.at[direction, i], recv_sem=halo_recv.at[direction, i],
            device_id=(c, target), device_id_type=MESH,
        )

    def send_halo(i):
        @pl.when(t > 0)
        def _():
            halo(0, i).start()

        @pl.when(t < n_tile - 1)
        def _():
            halo(1, i).start()

    send_halo(0)

    def pack_on(k, carry):
        pack(k)
        send_halo(k)
        return carry

    lax.fori_loop(1, nk, pack_on, 0)

    arow, acol = iota((m, m), 0), iota((m, m), 1)
    same = lax.div(arow, rows) == lax.div(acol, rows)
    amat[0] = banded(jnp.abs(arow - acol), same, hi)
    amat[1] = banded(jnp.abs(arow - acol), same, lo)
    brow, bcol = iota((m, 64), 0), iota((m, 64), 1)
    inner = lax.rem(bcol, 16)
    place = lax.rem(inner, 2) + jnp.where(lax.rem(bcol, 32) >= 16, rows, -2)
    same = lax.div(inner, 2) == lax.div(brow, rows)
    dist = jnp.abs(lax.rem(brow, rows) - place)
    bmat[...] = jnp.where(bcol < 32, banded(dist, same, hi).astype(F32), banded(dist, same, lo).astype(F32)).astype(BF16)

    @pl.when(t == 0)
    def _():
        top_in[...] = jnp.zeros_like(top_in)

    @pl.when(t == n_tile - 1)
    def _():
        bot_in[...] = jnp.zeros_like(bot_in)

    @pl.when(c == 0)
    def _():
        zs[0] = jnp.zeros((rows, cols), F32)

    @pl.when(c == n_chan - 1)
    def _():
        zs[nch + 1] = jnp.zeros((rows, cols), F32)

    def wait_halo(i):
        @pl.when(t < n_tile - 1)
        def _():
            halo(0, i).wait_recv()

        @pl.when(t > 0)
        def _():
            halo(1, i).wait_recv()

    def row_pass(k):
        wait_halo(k)
        x = x_ref[pl.ds(k * KC, KC)].reshape(m, cols)
        part = pl.ds(pl.multiple_of(k * 16, 16), 16)
        rim = jnp.concatenate([top_in[part, :], bot_in[part, :]] * 2, axis=0)
        z = jnp.dot(amat[0], x, preferred_element_type=F32)
        z += jnp.dot(amat[1], x, preferred_element_type=F32)
        z += jnp.dot(bmat[...], rim, preferred_element_type=F32)
        zs[pl.ds(k * KC + 1, KC)] = z.reshape(KC, rows, cols)

    def edge(direction):
        src, dst = (1, nch + 1) if direction == 0 else (nch, 0)
        target = lax.max(c - 1, 0) if direction == 0 else lax.min(c + 1, n_chan - 1)
        return pltpu.make_async_remote_copy(
            src_ref=zs.at[src], dst_ref=zs.at[dst],
            send_sem=edge_send.at[direction], recv_sem=edge_recv.at[direction],
            device_id=(target, t), device_id_type=MESH,
        )

    def data(slot, source, target, k):
        return pltpu.make_async_remote_copy(
            src_ref=stage.at[target, pl.ds(k * KC, KC)],
            dst_ref=out_ref.at[pl.ds(source * nch + k * KC, KC)],
            send_sem=data_send.at[slot, k], recv_sem=data_recv.at[source, k],
            device_id=(target, t), device_id_type=MESH,
        )

    lane = iota((rows, cols), 1)

    def finish(k):
        def one(i, carry):
            ch = k * KC + i
            h = 0.5 * zs[ch + 1] + 0.25 * (zs[ch] + zs[ch + 2])
            near = jnp.where(lane >= 1, pltpu.roll(h, 1, 1), 0.0) + jnp.where(
                lane < cols - 1, pltpu.roll(h, cols - 1, 1), 0.0
            )
            far = jnp.where(lane >= 2, pltpu.roll(h, 2, 1), 0.0) + jnp.where(
                lane < cols - 2, pltpu.roll(h, cols - 2, 1), 0.0
            )
            res = (taps[0] * h + taps[1] * near + taps[2] * far).astype(BF16)
            width = cols // n_chan
            for j in range(n_chan):
                stage[j, ch] = res[:, j * width : (j + 1) * width]
            return carry

        lax.fori_loop(0, KC, one, 0, unroll=2)
        for slot, p in enumerate(peers):
            data(slot, c, p, k).start()
        out_ref[pl.ds(c * nch + k * KC, KC)] = stage[c, pl.ds(k * KC, KC)]

    def first(k, carry):
        row_pass(k)
        return carry

    def both(k, carry):
        row_pass(k)
        finish(k - 1)
        return carry

    lax.fori_loop(0, 2, first, 0)

    @pl.when(c > 0)
    def _():
        edge(0).start()

    lax.fori_loop(2, nk, both, 0)

    @pl.when(c < n_chan - 1)
    def _():
        edge(1).start()

    @pl.when(c < n_chan - 1)
    def _():
        edge(0).wait_recv()

    @pl.when(c > 0)
    def _():
        edge(1).wait_recv()

    def last(i, carry):
        finish(i * (nk - 1))
        return carry

    lax.fori_loop(0, 2, last, 0)

    for copy in small:
        copy.wait()
    width = cols // n_chan
    per = width // BPIX
    r, l = iota((rows, width), 0), iota((rows, width), 1)
    group = lax.div(l, BPIX)
    turn = lax.rem(group - lax.rem(r, per) + per, per)
    for q in range(nq):
        tile_low[q] = jnp.zeros((rows, width), jnp.int32)
        tile_high[q] = jnp.zeros((rows, width), jnp.int32)
    picks = [pick_ref[0, 0, s] for s in range(send_count)]
    owners = [owner_ref[0, 0, s] for s in range(send_count)]
    sources = [source_ref[0, 0, s] for s in range(send_count)]
    slots = []
    for s in range(send_count):
        rank = jnp.int32(0)
        for e in range(s):
            rank = rank + jnp.where(owners[e] == owners[s], 1, 0)
        slots.append(owners[s] * CAP + rank)
    qs = [lax.div(p, per) for p in picks]
    vs = [lax.rem(p, per) for p in picks]
    for s in range(send_count):
        for ends_ref, grid in ((low_ref, tile_low), (high_ref, tile_high)):
            for a in range(rows // per):
                line = ends_ref[0, 0, pl.ds(s, 1), pl.ds(a * width, width)]
                rep[pl.ds(a * per, per), :] = jnp.broadcast_to(line, (per, width))
            base = rep[...]
            value = base
            for i in range(1, per):
                value = jnp.where(turn == i, pltpu.roll(base, i * BPIX, 1), value)
            for q in range(nq):
                hit = (group == vs[s]) & (qs[s] == q)
                grid[q] = jnp.where(hit, value, grid[q])

    entries = n_tile * CAP
    er = iota((entries, width), 0)
    eg = lax.div(iota((entries, width), 1), BPIX)
    tags = jnp.zeros((entries, width), F32)
    for q in range(nq):
        chosen = jnp.zeros((entries, width), F32)
        for s in range(send_count):
            chosen = jnp.where((er == slots[s]) & (eg == vs[s]) & (qs[s] == q), 1.0, chosen)
        pick_mat[q] = jnp.concatenate([chosen, chosen], axis=1).astype(BF16)
    for s in range(send_count):
        tags = jnp.where(er == slots[s], (sources[s] * nq + qs[s]).astype(F32), tags)
    for o in range(n_tile):
        msg[o, pl.ds(16, 8), :] = jnp.concatenate(
            [tags[o * CAP : o * CAP + CAP], jnp.zeros((6, width), F32)], axis=0
        )
    moments[...] = jnp.zeros_like(moments)
    chans = iota((KC, rows, width), 0)

    def measure(source, k):
        base = pl.multiple_of(source * nch + k * KC, KC)
        q = lax.div(base, BCH)
        v = out_ref[pl.ds(base, KC)].astype(F32)
        pos = chans + lax.rem(base, BCH)
        inside = (tile_low[q][None] <= pos) & (pos < tile_high[q][None])
        v = jnp.where(inside, v, 0.0)
        moments[q] += jnp.sum(v, axis=0)
        colsum[pl.ds(base, KC), :] = jnp.sum(v, axis=1)

    def order(i):
        return jnp.where(i < nk - 2, i + 1, jnp.where(i == nk - 2, 0, nk - 1))

    def own(k, carry):
        measure(c, k)
        return carry

    lax.fori_loop(0, nk, own, 0)

    def arrive_same(i, carry):
        k = order(i)
        data(len(peers) - 1, peers[-1], c, k).wait_recv()
        measure(peers[-1], k)
        return carry

    lax.fori_loop(0, nk, arrive_same, 0)

    def arrive(i, carry):
        k = order(i)
        for slot, p in enumerate(peers[:-1]):
            data(slot, p, c, k).wait_recv()
            measure(p, k)
        return carry

    lax.fori_loop(0, nk, arrive, 0)

    blocks = {}
    lines = iota((rows // per, width), 1)
    lane_group = lax.div(lines, BPIX)
    for q in range(nq):
        strips = [moments[q, pl.ds(j, rows // per, stride=per), :] for j in range(per)]
        for v in range(per):
            total = jnp.zeros((rows // per, width), F32)
            for j in range(per):
                turned = strips[j] if j == v else pltpu.roll(strips[j], (j - v) % per * BPIX, 1)
                total = jnp.where(lane_group == j, turned, total)
            blocks[q, v] = total
    maps = []
    for s in range(send_count):
        total = jnp.zeros((rows // per, width), F32)
        for (q, v), block in blocks.items():
            total = jnp.where(picks[s] == q * per + v, block, total)
        maps.append(total)
    spectra = jnp.zeros((entries, BCH), F32)
    for q in range(nq):
        sums = colsum[pl.ds(q * BCH, BCH), :]
        high = sums.astype(BF16)
        low = (sums - high.astype(F32)).astype(BF16)
        spectra += lax.dot_general(
            pick_mat[q], jnp.concatenate([high, low], axis=1), (((1,), (1,)), ((), ())),
            preferred_element_type=F32,
        )
    for o in range(n_tile):
        for n in range(CAP):
            total = jnp.zeros((rows // per, width), F32)
            for s in range(send_count):
                total = jnp.where(slots[s] == o * CAP + n, maps[s], total)
            msg[o, pl.ds(n * 8, 8), :] = total
        msg[o, pl.ds(16 + CAP, CAP), :] = spectra[o * CAP : o * CAP + CAP]

    def to_owner(d, source, target):
        return pltpu.make_async_remote_copy(
            src_ref=msg.at[target], dst_ref=rcv.at[source],
            send_sem=own_send.at[d], recv_sem=own_recv.at[source],
            device_id=(c, target), device_id_type=MESH,
        )

    for d, p in enumerate(tiles):
        to_owner(d, t, p).start()
    rcv[t] = msg[t]

    def halo_left(i, carry):
        @pl.when(t > 0)
        def _():
            halo(0, i).wait_send()

        @pl.when(t < n_tile - 1)
        def _():
            halo(1, i).wait_send()

        return carry

    lax.fori_loop(0, nk, halo_left, 0)

    @pl.when(c > 0)
    def _():
        edge(0).wait_send()

    @pl.when(c < n_chan - 1)
    def _():
        edge(1).wait_send()

    def left(k, carry):
        for slot, p in enumerate(peers):
            data(slot, c, p, k).wait_send()
        return carry

    lax.fori_loop(0, nk, left, 0)
    for d, p in enumerate(tiles):
        to_owner(d, t, p).wait_send()
    for d, p in enumerate(tiles):
        to_owner(d, p, p).wait_recv()

    maps_ref[...] = rcv[:, :16, :]
    which = iota((SRC_DEV, width), 0) * nq
    totals = [jnp.zeros((SRC_DEV, BCH), F32) for _ in range(nq)]
    for i in range(n_tile):
        for n in range(CAP):
            line = rcv[i, pl.ds(18 + n, 1), :]
            tag = rcv[i, pl.ds(16 + n, 1), :]
            for q in range(nq):
                totals[q] = totals[q] + jnp.where(tag == (which + q).astype(F32), line, 0.0)
    for q in range(nq):
        spec_ref[:, pl.ds(q * BCH, BCH)] = totals[q]


def solution(mesh):
    n_chan, n_tile = mesh.shape["chan"], mesh.shape["tile"]

    def step(intensity, block_pick, owner_tile, source_index, mask_low, mask_high):
        nch, rows, cols = intensity.shape
        width = cols // n_chan
        send_count = block_pick.shape[-1]
        total = nch * n_chan
        nq = total // BCH
        nk = nch // KC
        vmem = pl.BlockSpec(memory_space=pltpu.VMEM)
        hbm = pl.BlockSpec(memory_space=pltpu.HBM)
        dma = pltpu.SemaphoreType.DMA
        maps, spectra, smoothed = pl.pallas_call(
            functools.partial(kernel, n_chan, n_tile, send_count),
            out_shape=(
                jax.ShapeDtypeStruct((n_tile, CAP * 8, 128), F32),
                jax.ShapeDtypeStruct((SRC_DEV, total), F32),
                jax.ShapeDtypeStruct((total, rows, width), BF16),
            ),
            in_specs=[hbm] * 6,
            out_specs=(vmem, vmem, vmem),
            scratch_shapes=[
                pltpu.VMEM((nch, rows, cols), BF16),
                pltpu.SMEM((1, 1, send_count), jnp.int32),
                pltpu.SMEM((1, 1, send_count), jnp.int32),
                pltpu.SMEM((1, 1, send_count), jnp.int32),
                pltpu.VMEM((1, 1, send_count, 8 * 128), jnp.int32),
                pltpu.VMEM((1, 1, send_count, 8 * 128), jnp.int32),
                pltpu.VMEM((2, KC * rows, KC * rows), BF16),
                pltpu.VMEM((KC * rows, 64), BF16),
                pltpu.VMEM((nch * 2, cols), BF16),
                pltpu.VMEM((nch * 2, cols), BF16),
                pltpu.VMEM((nch * 2, cols), BF16),
                pltpu.VMEM((nch * 2, cols), BF16),
                pltpu.VMEM((nch + 2, rows, cols), F32),
                pltpu.VMEM((n_chan, nch, rows, width), BF16),
                pltpu.VMEM((nq, rows, width), jnp.int32),
                pltpu.VMEM((nq, rows, width), jnp.int32),
                pltpu.VMEM((rows, width), jnp.int32),
                pltpu.VMEM((nq, rows, width), F32),
                pltpu.VMEM((total, width), F32),
                pltpu.VMEM((n_tile, 24, width), F32),
                pltpu.VMEM((n_tile, 24, width), F32),
                pltpu.VMEM((nq, n_tile * CAP, 2 * width), BF16),
                dma((nk,)), dma((5,)), dma((2, nk)), dma((2, nk)), dma((2,)), dma((2,)),
                dma((n_chan - 1, nk)), dma((n_chan, nk)),
                dma((n_tile - 1,)), dma((n_tile,)),
            ],
            compiler_params=pltpu.CompilerParams(
                collective_id=0, has_side_effects=True, vmem_limit_bytes=49152 * 1024
            ),
        )(*[pltpu.with_memory_space_constraint(v, pltpu.HBM) for v in (intensity, block_pick, owner_tile, source_index, mask_low, mask_high)])
        return (
            maps.reshape(1, 1, n_tile, CAP, 8 * 128),
            spectra.reshape(1, 1, SRC_DEV, total),
            smoothed,
        )

    return jax.shard_map(
        step,
        mesh=mesh,
        in_specs=(
            P("chan", "tile", None),
            P("tile", "chan", None),
            P("tile", "chan", None),
            P("tile", "chan", None),
            P("tile", "chan", None, None),
            P("tile", "chan", None, None),
        ),
        out_specs=(
            P("tile", "chan", None, None, None),
            P("tile", "chan", None, None),
            P(None, "tile", "chan"),
        ),
        check_vma=False,
    )
```

```python
import functools

import jax
import jax.numpy as jnp
import numpy as np
from jax import lax
from jax.experimental import pallas as pl
from jax.experimental.pallas import tpu as pltpu
from jax.sharding import PartitionSpec as P

BCH = 128
BPIX = 32
CAP = 2
SRC_DEV = 16
SIGMA = 1.5
KC = 8
MESH = pl.DeviceIdType.MESH
F32 = jnp.float32
BF16 = jnp.bfloat16


def gauss_taps():
    off = np.arange(-2, 3).astype(np.float32)
    raw = np.exp(-off * off / np.float32(2.0 * SIGMA * SIGMA))
    g = (raw / raw.sum()).astype(np.float32)
    return [float(g[2]), float(g[3]), float(g[4])]


def split_taps(taps):
    hi = [float(np.float32(np.asarray(v, dtype=jnp.bfloat16))) for v in taps]
    lo = [v - h for v, h in zip(taps, hi)]
    return hi, lo


def banded(dist, same, taps):
    value = jnp.where(dist == 0, taps[0], jnp.where(dist == 1, taps[1], jnp.where(dist == 2, taps[2], 0.0)))
    return jnp.where(same, value, 0.0).astype(BF16)


def iota(shape, dim):
    return lax.broadcasted_iota(jnp.int32, shape, dim)


def kernel(
    n_chan, n_tile, send_count,
    x_hbm, pick_hbm, owner_hbm, source_hbm, low_hbm, high_hbm,
    maps_ref, spec_ref, out_ref,
    x_ref, pick_ref, owner_ref, source_ref, low_ref, high_ref,
    amat, bmat, up_out, dn_out, top_in, bot_in, zs, stage, tile_low, tile_high, rep,
    moments, colsum, msg, rcv, pick_mat,
    x_sem, arg_sem, halo_send, halo_recv, edge_send, edge_recv, data_send, data_recv, own_send, own_recv,
):
    t = lax.axis_index("tile")
    c = lax.axis_index("chan")
    nch, rows, cols = x_ref.shape
    nk = nch // KC
    nq = n_chan * nch // BCH
    ny = n_chan // 2
    taps = gauss_taps()
    hi, lo = split_taps(taps)
    yy, core = c // 2, c % 2
    peers = []
    for dy in range(1, ny):
        for dc in range(2):
            peers.append(lax.rem(yy + dy, ny) * 2 + lax.rem(core + dc, 2))
    peers.append(yy * 2 + 1 - core)
    tiles = [lax.rem(t + d, n_tile) for d in range(1, n_tile)]

    def fetch(p):
        part = pl.ds(p * KC, KC)
        return pltpu.make_async_copy(x_hbm.at[part], x_ref.at[part], x_sem.at[p])

    small = [
        pltpu.make_async_copy(src, dst, arg_sem.at[i])
        for i, (src, dst) in enumerate((
            (pick_hbm, pick_ref), (owner_hbm, owner_ref), (source_hbm, source_ref),
            (low_hbm, low_ref), (high_hbm, high_ref),
        ))
    ]
    barrier = pltpu.get_barrier_semaphore()
    for p in peers:
        pl.semaphore_signal(barrier, inc=1, device_id=(p, t), device_id_type=MESH)
    for p in tiles:
        pl.semaphore_signal(barrier, inc=1, device_id=(c, p), device_id_type=MESH)

    for p in range(nk):
        fetch(p).start()
    for copy in small:
        copy.start()
    m = KC * rows

    srow, scol = iota((32, m), 0), iota((32, m), 1)
    within = lax.rem(srow, 16)
    wanted = lax.div(within, 2) * rows + lax.rem(within, 2) + jnp.where(srow >= 16, rows - 2, 0)
    select = jnp.where(scol == wanted, 1.0, 0.0).astype(BF16)

    def pack(k):
        fetch(k).wait()
        x = x_ref[pl.ds(k * KC, KC)].reshape(m, cols)
        picked = jnp.dot(select, x, preferred_element_type=F32).astype(BF16)
        up_out[pl.ds(pl.multiple_of(k * 16, 16), 16), :] = picked[:16]
        dn_out[pl.ds(pl.multiple_of(k * 16, 16), 16), :] = picked[16:]

    pack(0)
    pl.semaphore_wait(barrier, len(peers) + len(tiles))

    def halo(direction, i):
        part = pl.ds(i * 16, 16)
        src, dst = (up_out, bot_in) if direction == 0 else (dn_out, top_in)
        target = lax.max(t - 1, 0) if direction == 0 else lax.min(t + 1, n_tile - 1)
        return pltpu.make_async_remote_copy(
            src_ref=src.at[part, :], dst_ref=dst.at[part, :],
            send_sem=halo_send.at[direction, i], recv_sem=halo_recv.at[direction, i],
            device_id=(c, target), device_id_type=MESH,
        )

    def send_halo(i):
        @pl.when(t > 0)
        def _():
            halo(0, i).start()

        @pl.when(t < n_tile - 1)
        def _():
            halo(1, i).start()

    send_halo(0)

    def pack_on(k, carry):
        pack(k)
        send_halo(k)
        return carry

    ahead = min(4, nk)
    lax.fori_loop(1, ahead, pack_on, 0)

    arow, acol = iota((m, m), 0), iota((m, m), 1)
    same = lax.div(arow, rows) == lax.div(acol, rows)
    amat[0] = banded(jnp.abs(arow - acol), same, hi)
    amat[1] = banded(jnp.abs(arow - acol), same, lo)
    brow, bcol = iota((m, 64), 0), iota((m, 64), 1)
    inner = lax.rem(bcol, 16)
    place = lax.rem(inner, 2) + jnp.where(lax.rem(bcol, 32) >= 16, rows, -2)
    same = lax.div(inner, 2) == lax.div(brow, rows)
    dist = jnp.abs(lax.rem(brow, rows) - place)
    bmat[...] = jnp.where(bcol < 32, banded(dist, same, hi).astype(F32), banded(dist, same, lo).astype(F32)).astype(BF16)

    @pl.when(t == 0)
    def _():
        top_in[...] = jnp.zeros_like(top_in)

    @pl.when(t == n_tile - 1)
    def _():
        bot_in[...] = jnp.zeros_like(bot_in)

    @pl.when(c == 0)
    def _():
        zs[0] = jnp.zeros((rows, cols), F32)

    @pl.when(c == n_chan - 1)
    def _():
        zs[nch + 1] = jnp.zeros((rows, cols), F32)

    def wait_halo(i):
        @pl.when(t < n_tile - 1)
        def _():
            halo(0, i).wait_recv()

        @pl.when(t > 0)
        def _():
            halo(1, i).wait_recv()

    def row_pass(k):
        wait_halo(k)
        x = x_ref[pl.ds(k * KC, KC)].reshape(m, cols)
        part = pl.ds(pl.multiple_of(k * 16, 16), 16)
        rim = jnp.concatenate([top_in[part, :], bot_in[part, :]] * 2, axis=0)
        z = jnp.dot(amat[0], x, preferred_element_type=F32)
        z += jnp.dot(amat[1], x, preferred_element_type=F32)
        z += jnp.dot(bmat[...], rim, preferred_element_type=F32)
        zs[pl.ds(k * KC + 1, KC)] = z.reshape(KC, rows, cols)

    def edge(direction):
        src, dst = (1, nch + 1) if direction == 0 else (nch, 0)
        target = lax.max(c - 1, 0) if direction == 0 else lax.min(c + 1, n_chan - 1)
        return pltpu.make_async_remote_copy(
            src_ref=zs.at[src], dst_ref=zs.at[dst],
            send_sem=edge_send.at[direction], recv_sem=edge_recv.at[direction],
            device_id=(target, t), device_id_type=MESH,
        )

    def data(slot, source, target, k):
        return pltpu.make_async_remote_copy(
            src_ref=stage.at[target, pl.ds(k * KC, KC)],
            dst_ref=out_ref.at[pl.ds(source * nch + k * KC, KC)],
            send_sem=data_send.at[slot, k], recv_sem=data_recv.at[source, k],
            device_id=(target, t), device_id_type=MESH,
        )

    lane = iota((rows, cols), 1)

    def finish(k):
        def one(i, carry):
            ch = k * KC + i
            h = 0.5 * zs[ch + 1] + 0.25 * (zs[ch] + zs[ch + 2])
            near = jnp.where(lane >= 1, pltpu.roll(h, 1, 1), 0.0) + jnp.where(
                lane < cols - 1, pltpu.roll(h, cols - 1, 1), 0.0
            )
            far = jnp.where(lane >= 2, pltpu.roll(h, 2, 1), 0.0) + jnp.where(
                lane < cols - 2, pltpu.roll(h, cols - 2, 1), 0.0
            )
            res = (taps[0] * h + taps[1] * near + taps[2] * far).astype(BF16)
            width = cols // n_chan
            for j in range(n_chan):
                stage[j, ch] = res[:, j * width : (j + 1) * width]
            return carry

        lax.fori_loop(0, KC, one, 0, unroll=2)
        for slot, p in enumerate(peers):
            data(slot, c, p, k).start()
        out_ref[pl.ds(c * nch + k * KC, KC)] = stage[c, pl.ds(k * KC, KC)]

    def first(k, carry):
        row_pass(k)
        return carry

    def both(k, carry):
        row_pass(k)
        finish(k - 1)
        return carry

    lax.fori_loop(0, 2, first, 0)

    @pl.when(c > 0)
    def _():
        edge(0).start()

    def all_three(k, carry):
        pack_on(k + ahead - 2, carry)
        return both(k, carry)

    lax.fori_loop(2, nk - ahead + 2, all_three, 0)
    lax.fori_loop(nk - ahead + 2, nk, both, 0)

    @pl.when(c < n_chan - 1)
    def _():
        edge(1).start()

    @pl.when(c < n_chan - 1)
    def _():
        edge(0).wait_recv()

    @pl.when(c > 0)
    def _():
        edge(1).wait_recv()

    def last(i, carry):
        finish(i * (nk - 1))
        return carry

    lax.fori_loop(0, 2, last, 0)

    for copy in small:
        copy.wait()
    width = cols // n_chan
    per = width // BPIX
    r, l = iota((rows, width), 0), iota((rows, width), 1)
    group = lax.div(l, BPIX)
    turn = lax.rem(group - lax.rem(r, per) + per, per)
    for q in range(nq):
        tile_low[q] = jnp.zeros((rows, width), jnp.int32)
        tile_high[q] = jnp.zeros((rows, width), jnp.int32)
    picks = [pick_ref[0, 0, s] for s in range(send_count)]
    owners = [owner_ref[0, 0, s] for s in range(send_count)]
    sources = [source_ref[0, 0, s] for s in range(send_count)]
    slots = []
    for s in range(send_count):
        rank = jnp.int32(0)
        for e in range(s):
            rank = rank + jnp.where(owners[e] == owners[s], 1, 0)
        slots.append(owners[s] * CAP + rank)
    qs = [lax.div(p, per) for p in picks]
    vs = [lax.rem(p, per) for p in picks]
    for s in range(send_count):
        for ends_ref, grid in ((low_ref, tile_low), (high_ref, tile_high)):
            for a in range(rows // per):
                line = ends_ref[0, 0, pl.ds(s, 1), pl.ds(a * width, width)]
                rep[pl.ds(a * per, per), :] = jnp.broadcast_to(line, (per, width))
            base = rep[...]
            value = base
            for i in range(1, per):
                value = jnp.where(turn == i, pltpu.roll(base, i * BPIX, 1), value)
            for q in range(nq):
                hit = (group == vs[s]) & (qs[s] == q)
                grid[q] = jnp.where(hit, value, grid[q])

    entries = n_tile * CAP
    er = iota((entries, width), 0)
    eg = lax.div(iota((entries, width), 1), BPIX)
    tags = jnp.zeros((entries, width), F32)
    for q in range(nq):
        chosen = jnp.zeros((entries, width), F32)
        for s in range(send_count):
            chosen = jnp.where((er == slots[s]) & (eg == vs[s]) & (qs[s] == q), 1.0, chosen)
        pick_mat[q] = jnp.concatenate([chosen, chosen], axis=1).astype(BF16)
    for s in range(send_count):
        tags = jnp.where(er == slots[s], (sources[s] * nq + qs[s]).astype(F32), tags)
    for o in range(n_tile):
        msg[o, pl.ds(16, 8), :] = jnp.concatenate(
            [tags[o * CAP : o * CAP + CAP], jnp.zeros((6, width), F32)], axis=0
        )
    moments[...] = jnp.zeros_like(moments)
    chans = iota((KC, rows, width), 0)

    def measure(source, k):
        base = pl.multiple_of(source * nch + k * KC, KC)
        q = lax.div(base, BCH)
        v = out_ref[pl.ds(base, KC)].astype(F32)
        pos = chans + lax.rem(base, BCH)
        inside = (tile_low[q][None] <= pos) & (pos < tile_high[q][None])
        v = jnp.where(inside, v, 0.0)
        moments[q] += jnp.sum(v, axis=0)
        colsum[pl.ds(base, KC), :] = jnp.sum(v, axis=1)

    def order(i):
        return jnp.where(i < nk - 2, i + 1, jnp.where(i == nk - 2, 0, nk - 1))

    def own(k, carry):
        measure(c, k)
        return carry

    lax.fori_loop(0, nk, own, 0)

    def arrive_same(i, carry):
        k = order(i)
        data(len(peers) - 1, peers[-1], c, k).wait_recv()
        measure(peers[-1], k)
        return carry

    lax.fori_loop(0, nk, arrive_same, 0)

    def arrive(i, carry):
        k = order(i)
        for slot, p in enumerate(peers[:-1]):
            data(slot, p, c, k).wait_recv()
            measure(p, k)
        return carry

    lax.fori_loop(0, nk, arrive, 0)

    blocks = {}
    lines = iota((rows // per, width), 1)
    lane_group = lax.div(lines, BPIX)
    for q in range(nq):
        strips = [moments[q, pl.ds(j, rows // per, stride=per), :] for j in range(per)]
        for v in range(per):
            total = jnp.zeros((rows // per, width), F32)
            for j in range(per):
                turned = strips[j] if j == v else pltpu.roll(strips[j], (j - v) % per * BPIX, 1)
                total = jnp.where(lane_group == j, turned, total)
            blocks[q, v] = total
    maps = []
    for s in range(send_count):
        total = jnp.zeros((rows // per, width), F32)
        for (q, v), block in blocks.items():
            total = jnp.where(picks[s] == q * per + v, block, total)
        maps.append(total)
    spectra = jnp.zeros((entries, BCH), F32)
    for q in range(nq):
        sums = colsum[pl.ds(q * BCH, BCH), :]
        high = sums.astype(BF16)
        low = (sums - high.astype(F32)).astype(BF16)
        spectra += lax.dot_general(
            pick_mat[q], jnp.concatenate([high, low], axis=1), (((1,), (1,)), ((), ())),
            preferred_element_type=F32,
        )
    for o in range(n_tile):
        for n in range(CAP):
            total = jnp.zeros((rows // per, width), F32)
            for s in range(send_count):
                total = jnp.where(slots[s] == o * CAP + n, maps[s], total)
            msg[o, pl.ds(n * 8, 8), :] = total
        msg[o, pl.ds(16 + CAP, CAP), :] = spectra[o * CAP : o * CAP + CAP]

    def to_owner(d, source, target):
        return pltpu.make_async_remote_copy(
            src_ref=msg.at[target], dst_ref=rcv.at[source],
            send_sem=own_send.at[d], recv_sem=own_recv.at[source],
            device_id=(c, target), device_id_type=MESH,
        )

    for d, p in enumerate(tiles):
        to_owner(d, t, p).start()
    rcv[t] = msg[t]

    def halo_left(i, carry):
        @pl.when(t > 0)
        def _():
            halo(0, i).wait_send()

        @pl.when(t < n_tile - 1)
        def _():
            halo(1, i).wait_send()

        return carry

    lax.fori_loop(0, nk, halo_left, 0)

    @pl.when(c > 0)
    def _():
        edge(0).wait_send()

    @pl.when(c < n_chan - 1)
    def _():
        edge(1).wait_send()

    def left(k, carry):
        for slot, p in enumerate(peers):
            data(slot, c, p, k).wait_send()
        return carry

    lax.fori_loop(0, nk, left, 0)
    for d, p in enumerate(tiles):
        to_owner(d, t, p).wait_send()
    for d, p in enumerate(tiles):
        to_owner(d, p, p).wait_recv()

    maps_ref[...] = rcv[:, :16, :]
    which = iota((SRC_DEV, width), 0) * nq
    totals = [jnp.zeros((SRC_DEV, BCH), F32) for _ in range(nq)]
    for i in range(n_tile):
        for n in range(CAP):
            line = rcv[i, pl.ds(18 + n, 1), :]
            tag = rcv[i, pl.ds(16 + n, 1), :]
            for q in range(nq):
                totals[q] = totals[q] + jnp.where(tag == (which + q).astype(F32), line, 0.0)
    for q in range(nq):
        spec_ref[:, pl.ds(q * BCH, BCH)] = totals[q]


def solution(mesh):
    n_chan, n_tile = mesh.shape["chan"], mesh.shape["tile"]

    def step(intensity, block_pick, owner_tile, source_index, mask_low, mask_high):
        nch, rows, cols = intensity.shape
        width = cols // n_chan
        send_count = block_pick.shape[-1]
        total = nch * n_chan
        nq = total // BCH
        nk = nch // KC
        vmem = pl.BlockSpec(memory_space=pltpu.VMEM)
        hbm = pl.BlockSpec(memory_space=pltpu.HBM)
        dma = pltpu.SemaphoreType.DMA
        maps, spectra, smoothed = pl.pallas_call(
            functools.partial(kernel, n_chan, n_tile, send_count),
            out_shape=(
                jax.ShapeDtypeStruct((n_tile, CAP * 8, 128), F32),
                jax.ShapeDtypeStruct((SRC_DEV, total), F32),
                jax.ShapeDtypeStruct((total, rows, width), BF16),
            ),
            in_specs=[hbm] * 6,
            out_specs=(vmem, vmem, vmem),
            scratch_shapes=[
                pltpu.VMEM((nch, rows, cols), BF16),
                pltpu.SMEM((1, 1, send_count), jnp.int32),
                pltpu.SMEM((1, 1, send_count), jnp.int32),
                pltpu.SMEM((1, 1, send_count), jnp.int32),
                pltpu.VMEM((1, 1, send_count, 8 * 128), jnp.int32),
                pltpu.VMEM((1, 1, send_count, 8 * 128), jnp.int32),
                pltpu.VMEM((2, KC * rows, KC * rows), BF16),
                pltpu.VMEM((KC * rows, 64), BF16),
                pltpu.VMEM((nch * 2, cols), BF16),
                pltpu.VMEM((nch * 2, cols), BF16),
                pltpu.VMEM((nch * 2, cols), BF16),
                pltpu.VMEM((nch * 2, cols), BF16),
                pltpu.VMEM((nch + 2, rows, cols), F32),
                pltpu.VMEM((n_chan, nch, rows, width), BF16),
                pltpu.VMEM((nq, rows, width), jnp.int32),
                pltpu.VMEM((nq, rows, width), jnp.int32),
                pltpu.VMEM((rows, width), jnp.int32),
                pltpu.VMEM((nq, rows, width), F32),
                pltpu.VMEM((total, width), F32),
                pltpu.VMEM((n_tile, 24, width), F32),
                pltpu.VMEM((n_tile, 24, width), F32),
                pltpu.VMEM((nq, n_tile * CAP, 2 * width), BF16),
                dma((nk,)), dma((5,)), dma((2, nk)), dma((2, nk)), dma((2,)), dma((2,)),
                dma((n_chan - 1, nk)), dma((n_chan, nk)),
                dma((n_tile - 1,)), dma((n_tile,)),
            ],
            compiler_params=pltpu.CompilerParams(
                collective_id=0, has_side_effects=True, vmem_limit_bytes=49152 * 1024
            ),
        )(*[pltpu.with_memory_space_constraint(v, pltpu.HBM) for v in (intensity, block_pick, owner_tile, source_index, mask_low, mask_high)])
        return (
            maps.reshape(1, 1, n_tile, CAP, 8 * 128),
            spectra.reshape(1, 1, SRC_DEV, total),
            smoothed,
        )

    return jax.shard_map(
        step,
        mesh=mesh,
        in_specs=(
            P("chan", "tile", None),
            P("tile", "chan", None),
            P("tile", "chan", None),
            P("tile", "chan", None),
            P("tile", "chan", None, None),
            P("tile", "chan", None, None),
        ),
        out_specs=(
            P("tile", "chan", None, None, None),
            P("tile", "chan", None, None),
            P(None, "tile", "chan"),
        ),
        check_vma=False,
    )
```

```python
import functools

import jax
import jax.numpy as jnp
import numpy as np
from jax import lax
from jax.experimental import pallas as pl
from jax.experimental.pallas import tpu as pltpu
from jax.sharding import PartitionSpec as P

BCH = 128
BPIX = 32
CAP = 2
SRC_DEV = 16
SIGMA = 1.5
KC = 8
MESH = pl.DeviceIdType.MESH
F32 = jnp.float32
BF16 = jnp.bfloat16


def gauss_taps():
    off = np.arange(-2, 3).astype(np.float32)
    raw = np.exp(-off * off / np.float32(2.0 * SIGMA * SIGMA))
    g = (raw / raw.sum()).astype(np.float32)
    return [float(g[2]), float(g[3]), float(g[4])]


def split_taps(taps):
    hi = [float(np.float32(np.asarray(v, dtype=jnp.bfloat16))) for v in taps]
    lo = [v - h for v, h in zip(taps, hi)]
    return hi, lo


def banded(dist, same, taps):
    value = jnp.where(dist == 0, taps[0], jnp.where(dist == 1, taps[1], jnp.where(dist == 2, taps[2], 0.0)))
    return jnp.where(same, value, 0.0).astype(BF16)


def iota(shape, dim):
    return lax.broadcasted_iota(jnp.int32, shape, dim)


def kernel(
    n_chan, n_tile, send_count,
    x_hbm, pick_hbm, owner_hbm, source_hbm, low_hbm, high_hbm,
    maps_ref, spec_ref, out_ref,
    x_ref, pick_ref, owner_ref, source_ref, low_ref, high_ref,
    amat, bmat, up_out, dn_out, top_in, bot_in, zs, stage, tile_low, tile_high, rep,
    moments, colsum, msg, rcv, pick_mat,
    x_sem, arg_sem, halo_send, halo_recv, edge_send, edge_recv, data_send, data_recv, own_send, own_recv,
):
    t = lax.axis_index("tile")
    c = lax.axis_index("chan")
    nch, rows, cols = x_ref.shape
    nk = nch // KC
    nq = n_chan * nch // BCH
    ny = n_chan // 2
    taps = gauss_taps()
    hi, lo = split_taps(taps)
    yy, core = c // 2, c % 2
    peers = []
    for dy in range(1, ny):
        for dc in range(2):
            peers.append(lax.rem(yy + dy, ny) * 2 + lax.rem(core + dc, 2))
    peers.append(yy * 2 + 1 - core)
    tiles = [lax.rem(t + d, n_tile) for d in range(1, n_tile)]

    def fetch(p):
        part = pl.ds(p * KC, KC)
        return pltpu.make_async_copy(x_hbm.at[part], x_ref.at[part], x_sem.at[p])

    small = [
        pltpu.make_async_copy(src, dst, arg_sem.at[i])
        for i, (src, dst) in enumerate((
            (pick_hbm, pick_ref), (owner_hbm, owner_ref), (source_hbm, source_ref),
            (low_hbm, low_ref), (high_hbm, high_ref),
        ))
    ]
    barrier = pltpu.get_barrier_semaphore()
    for p in peers:
        pl.semaphore_signal(barrier, inc=1, device_id=(p, t), device_id_type=MESH)
    for p in tiles:
        pl.semaphore_signal(barrier, inc=1, device_id=(c, p), device_id_type=MESH)

    for p in range(nk):
        fetch(p).start()
    for copy in small:
        copy.start()
    m = KC * rows

    srow, scol = iota((32, m), 0), iota((32, m), 1)
    within = lax.rem(srow, 16)
    wanted = lax.div(within, 2) * rows + lax.rem(within, 2) + jnp.where(srow >= 16, rows - 2, 0)
    select = jnp.where(scol == wanted, 1.0, 0.0).astype(BF16)

    def pack(k):
        fetch(k).wait()
        x = x_ref[pl.ds(k * KC, KC)].reshape(m, cols)
        picked = jnp.dot(select, x, preferred_element_type=F32).astype(BF16)
        up_out[pl.ds(pl.multiple_of(k * 16, 16), 16), :] = picked[:16]
        dn_out[pl.ds(pl.multiple_of(k * 16, 16), 16), :] = picked[16:]

    pack(0)
    pl.semaphore_wait(barrier, len(peers) + len(tiles))

    def halo(direction, i):
        part = pl.ds(i * 16, 16)
        src, dst = (up_out, bot_in) if direction == 0 else (dn_out, top_in)
        target = lax.max(t - 1, 0) if direction == 0 else lax.min(t + 1, n_tile - 1)
        return pltpu.make_async_remote_copy(
            src_ref=src.at[part, :], dst_ref=dst.at[part, :],
            send_sem=halo_send.at[direction, i], recv_sem=halo_recv.at[direction, i],
            device_id=(c, target), device_id_type=MESH,
        )

    def send_halo(i):
        @pl.when(t > 0)
        def _():
            halo(0, i).start()

        @pl.when(t < n_tile - 1)
        def _():
            halo(1, i).start()

    send_halo(0)

    def pack_on(k, carry):
        pack(k)
        send_halo(k)
        return carry

    ahead = min(3, nk)
    lax.fori_loop(1, ahead, pack_on, 0)

    arow, acol = iota((m, m), 0), iota((m, m), 1)
    same = lax.div(arow, rows) == lax.div(acol, rows)
    amat[0] = banded(jnp.abs(arow - acol), same, hi)
    amat[1] = banded(jnp.abs(arow - acol), same, lo)
    brow, bcol = iota((m, 64), 0), iota((m, 64), 1)
    inner = lax.rem(bcol, 16)
    place = lax.rem(inner, 2) + jnp.where(lax.rem(bcol, 32) >= 16, rows, -2)
    same = lax.div(inner, 2) == lax.div(brow, rows)
    dist = jnp.abs(lax.rem(brow, rows) - place)
    bmat[...] = jnp.where(bcol < 32, banded(dist, same, hi).astype(F32), banded(dist, same, lo).astype(F32)).astype(BF16)

    @pl.when(t == 0)
    def _():
        top_in[...] = jnp.zeros_like(top_in)

    @pl.when(t == n_tile - 1)
    def _():
        bot_in[...] = jnp.zeros_like(bot_in)

    @pl.when(c == 0)
    def _():
        zs[0] = jnp.zeros((rows, cols), F32)

    @pl.when(c == n_chan - 1)
    def _():
        zs[nch + 1] = jnp.zeros((rows, cols), F32)

    def wait_halo(i):
        @pl.when(t < n_tile - 1)
        def _():
            halo(0, i).wait_recv()

        @pl.when(t > 0)
        def _():
            halo(1, i).wait_recv()

    def row_pass(k):
        wait_halo(k)
        x = x_ref[pl.ds(k * KC, KC)].reshape(m, cols)
        part = pl.ds(pl.multiple_of(k * 16, 16), 16)
        rim = jnp.concatenate([top_in[part, :], bot_in[part, :]] * 2, axis=0)
        z = jnp.dot(amat[0], x, preferred_element_type=F32)
        z += jnp.dot(amat[1], x, preferred_element_type=F32)
        z += jnp.dot(bmat[...], rim, preferred_element_type=F32)
        zs[pl.ds(k * KC + 1, KC)] = z.reshape(KC, rows, cols)

    def edge(direction):
        src, dst = (1, nch + 1) if direction == 0 else (nch, 0)
        target = lax.max(c - 1, 0) if direction == 0 else lax.min(c + 1, n_chan - 1)
        return pltpu.make_async_remote_copy(
            src_ref=zs.at[src], dst_ref=zs.at[dst],
            send_sem=edge_send.at[direction], recv_sem=edge_recv.at[direction],
            device_id=(target, t), device_id_type=MESH,
        )

    def data(slot, source, target, k):
        return pltpu.make_async_remote_copy(
            src_ref=stage.at[target, pl.ds(k * KC, KC)],
            dst_ref=out_ref.at[pl.ds(source * nch + k * KC, KC)],
            send_sem=data_send.at[slot, k], recv_sem=data_recv.at[source, k],
            device_id=(target, t), device_id_type=MESH,
        )

    lane = iota((rows, cols), 1)

    def finish(k):
        def one(i, carry):
            ch = k * KC + i
            h = 0.5 * zs[ch + 1] + 0.25 * (zs[ch] + zs[ch + 2])
            near = jnp.where(lane >= 1, pltpu.roll(h, 1, 1), 0.0) + jnp.where(
                lane < cols - 1, pltpu.roll(h, cols - 1, 1), 0.0
            )
            far = jnp.where(lane >= 2, pltpu.roll(h, 2, 1), 0.0) + jnp.where(
                lane < cols - 2, pltpu.roll(h, cols - 2, 1), 0.0
            )
            res = (taps[0] * h + taps[1] * near + taps[2] * far).astype(BF16)
            width = cols // n_chan
            for j in range(n_chan):
                stage[j, ch] = res[:, j * width : (j + 1) * width]
            return carry

        lax.fori_loop(0, KC, one, 0, unroll=2)
        for slot, p in enumerate(peers[:-1]):
            data(slot, c, p, k).start()
        out_ref[pl.ds(c * nch + k * KC, KC)] = stage[c, pl.ds(k * KC, KC)]

    def first(k, carry):
        row_pass(k)
        return carry

    def both(k, carry):
        row_pass(k)
        finish(k - 1)
        return carry

    lax.fori_loop(0, 2, first, 0)

    @pl.when(c > 0)
    def _():
        edge(0).start()

    def all_three(k, carry):
        pack_on(k + ahead - 2, carry)
        return both(k, carry)

    lax.fori_loop(2, nk - ahead + 2, all_three, 0)
    lax.fori_loop(nk - ahead + 2, nk, both, 0)

    @pl.when(c < n_chan - 1)
    def _():
        edge(1).start()

    @pl.when(c < n_chan - 1)
    def _():
        edge(0).wait_recv()

    @pl.when(c > 0)
    def _():
        edge(1).wait_recv()

    def last(i, carry):
        finish(i * (nk - 1))
        return carry

    lax.fori_loop(0, 2, last, 0)

    def beside(k, carry):
        data(len(peers) - 1, c, peers[-1], k).start()
        return carry

    lax.fori_loop(0, nk, beside, 0)

    for copy in small:
        copy.wait()
    width = cols // n_chan
    per = width // BPIX
    r, l = iota((rows, width), 0), iota((rows, width), 1)
    group = lax.div(l, BPIX)
    turn = lax.rem(group - lax.rem(r, per) + per, per)
    for q in range(nq):
        tile_low[q] = jnp.zeros((rows, width), jnp.int32)
        tile_high[q] = jnp.zeros((rows, width), jnp.int32)
    picks = [pick_ref[0, 0, s] for s in range(send_count)]
    owners = [owner_ref[0, 0, s] for s in range(send_count)]
    sources = [source_ref[0, 0, s] for s in range(send_count)]
    slots = []
    for s in range(send_count):
        rank = jnp.int32(0)
        for e in range(s):
            rank = rank + jnp.where(owners[e] == owners[s], 1, 0)
        slots.append(owners[s] * CAP + rank)
    qs = [lax.div(p, per) for p in picks]
    vs = [lax.rem(p, per) for p in picks]
    for s in range(send_count):
        for ends_ref, grid in ((low_ref, tile_low), (high_ref, tile_high)):
            for a in range(rows // per):
                line = ends_ref[0, 0, pl.ds(s, 1), pl.ds(a * width, width)]
                rep[pl.ds(a * per, per), :] = jnp.broadcast_to(line, (per, width))
            base = rep[...]
            value = base
            for i in range(1, per):
                value = jnp.where(turn == i, pltpu.roll(base, i * BPIX, 1), value)
            for q in range(nq):
                hit = (group == vs[s]) & (qs[s] == q)
                grid[q] = jnp.where(hit, value, grid[q])

    entries = n_tile * CAP
    er = iota((entries, width), 0)
    eg = lax.div(iota((entries, width), 1), BPIX)
    tags = jnp.zeros((entries, width), F32)
    for q in range(nq):
        chosen = jnp.zeros((entries, width), F32)
        for s in range(send_count):
            chosen = jnp.where((er == slots[s]) & (eg == vs[s]) & (qs[s] == q), 1.0, chosen)
        pick_mat[q] = jnp.concatenate([chosen, chosen], axis=1).astype(BF16)
    for s in range(send_count):
        tags = jnp.where(er == slots[s], (sources[s] * nq + qs[s]).astype(F32), tags)
    for o in range(n_tile):
        msg[o, pl.ds(16, 8), :] = jnp.concatenate(
            [tags[o * CAP : o * CAP + CAP], jnp.zeros((6, width), F32)], axis=0
        )
    moments[...] = jnp.zeros_like(moments)
    chans = iota((KC, rows, width), 0)

    def measure(source, k):
        base = pl.multiple_of(source * nch + k * KC, KC)
        q = lax.div(base, BCH)
        v = out_ref[pl.ds(base, KC)].astype(F32)
        pos = chans + lax.rem(base, BCH)
        inside = (tile_low[q][None] <= pos) & (pos < tile_high[q][None])
        v = jnp.where(inside, v, 0.0)
        moments[q] += jnp.sum(v, axis=0)
        colsum[pl.ds(base, KC), :] = jnp.sum(v, axis=1)

    def order(i):
        return jnp.where(i < nk - 2, i + 1, jnp.where(i == nk - 2, 0, nk - 1))

    def own(k, carry):
        measure(c, k)
        return carry

    lax.fori_loop(0, nk, own, 0)

    def arrive_same(i, carry):
        k = order(i)
        data(len(peers) - 1, peers[-1], c, k).wait_recv()
        measure(peers[-1], k)
        return carry

    lax.fori_loop(0, nk, arrive_same, 0)

    def arrive(i, carry):
        k = order(i)
        for slot, p in enumerate(peers[:-1]):
            data(slot, p, c, k).wait_recv()
            measure(p, k)
        return carry

    lax.fori_loop(0, nk, arrive, 0)

    blocks = {}
    lines = iota((rows // per, width), 1)
    lane_group = lax.div(lines, BPIX)
    for q in range(nq):
        strips = [moments[q, pl.ds(j, rows // per, stride=per), :] for j in range(per)]
        for v in range(per):
            total = jnp.zeros((rows // per, width), F32)
            for j in range(per):
                turned = strips[j] if j == v else pltpu.roll(strips[j], (j - v) % per * BPIX, 1)
                total = jnp.where(lane_group == j, turned, total)
            blocks[q, v] = total
    maps = []
    for s in range(send_count):
        total = jnp.zeros((rows // per, width), F32)
        for (q, v), block in blocks.items():
            total = jnp.where(picks[s] == q * per + v, block, total)
        maps.append(total)
    spectra = jnp.zeros((entries, BCH), F32)
    for q in range(nq):
        sums = colsum[pl.ds(q * BCH, BCH), :]
        high = sums.astype(BF16)
        low = (sums - high.astype(F32)).astype(BF16)
        spectra += lax.dot_general(
            pick_mat[q], jnp.concatenate([high, low], axis=1), (((1,), (1,)), ((), ())),
            preferred_element_type=F32,
        )
    for o in range(n_tile):
        for n in range(CAP):
            total = jnp.zeros((rows // per, width), F32)
            for s in range(send_count):
                total = jnp.where(slots[s] == o * CAP + n, maps[s], total)
            msg[o, pl.ds(n * 8, 8), :] = total
        msg[o, pl.ds(16 + CAP, CAP), :] = spectra[o * CAP : o * CAP + CAP]

    def to_owner(d, source, target):
        return pltpu.make_async_remote_copy(
            src_ref=msg.at[target], dst_ref=rcv.at[source],
            send_sem=own_send.at[d], recv_sem=own_recv.at[source],
            device_id=(c, target), device_id_type=MESH,
        )

    for d, p in enumerate(tiles):
        to_owner(d, t, p).start()
    rcv[t] = msg[t]

    def halo_left(i, carry):
        @pl.when(t > 0)
        def _():
            halo(0, i).wait_send()

        @pl.when(t < n_tile - 1)
        def _():
            halo(1, i).wait_send()

        return carry

    lax.fori_loop(0, nk, halo_left, 0)

    @pl.when(c > 0)
    def _():
        edge(0).wait_send()

    @pl.when(c < n_chan - 1)
    def _():
        edge(1).wait_send()

    def left(k, carry):
        for slot, p in enumerate(peers):
            data(slot, c, p, k).wait_send()
        return carry

    lax.fori_loop(0, nk, left, 0)
    for d, p in enumerate(tiles):
        to_owner(d, t, p).wait_send()
    for d, p in enumerate(tiles):
        to_owner(d, p, p).wait_recv()

    maps_ref[...] = rcv[:, :16, :]
    which = iota((SRC_DEV, width), 0) * nq
    totals = [jnp.zeros((SRC_DEV, BCH), F32) for _ in range(nq)]
    for i in range(n_tile):
        for n in range(CAP):
            line = rcv[i, pl.ds(18 + n, 1), :]
            tag = rcv[i, pl.ds(16 + n, 1), :]
            for q in range(nq):
                totals[q] = totals[q] + jnp.where(tag == (which + q).astype(F32), line, 0.0)
    for q in range(nq):
        spec_ref[:, pl.ds(q * BCH, BCH)] = totals[q]


def solution(mesh):
    n_chan, n_tile = mesh.shape["chan"], mesh.shape["tile"]

    def step(intensity, block_pick, owner_tile, source_index, mask_low, mask_high):
        nch, rows, cols = intensity.shape
        width = cols // n_chan
        send_count = block_pick.shape[-1]
        total = nch * n_chan
        nq = total // BCH
        nk = nch // KC
        vmem = pl.BlockSpec(memory_space=pltpu.VMEM)
        hbm = pl.BlockSpec(memory_space=pltpu.HBM)
        dma = pltpu.SemaphoreType.DMA
        maps, spectra, smoothed = pl.pallas_call(
            functools.partial(kernel, n_chan, n_tile, send_count),
            out_shape=(
                jax.ShapeDtypeStruct((n_tile, CAP * 8, 128), F32),
                jax.ShapeDtypeStruct((SRC_DEV, total), F32),
                jax.ShapeDtypeStruct((total, rows, width), BF16),
            ),
            in_specs=[hbm] * 6,
            out_specs=(vmem, vmem, vmem),
            scratch_shapes=[
                pltpu.VMEM((nch, rows, cols), BF16),
                pltpu.SMEM((1, 1, send_count), jnp.int32),
                pltpu.SMEM((1, 1, send_count), jnp.int32),
                pltpu.SMEM((1, 1, send_count), jnp.int32),
                pltpu.VMEM((1, 1, send_count, 8 * 128), jnp.int32),
                pltpu.VMEM((1, 1, send_count, 8 * 128), jnp.int32),
                pltpu.VMEM((2, KC * rows, KC * rows), BF16),
                pltpu.VMEM((KC * rows, 64), BF16),
                pltpu.VMEM((nch * 2, cols), BF16),
                pltpu.VMEM((nch * 2, cols), BF16),
                pltpu.VMEM((nch * 2, cols), BF16),
                pltpu.VMEM((nch * 2, cols), BF16),
                pltpu.VMEM((nch + 2, rows, cols), F32),
                pltpu.VMEM((n_chan, nch, rows, width), BF16),
                pltpu.VMEM((nq, rows, width), jnp.int32),
                pltpu.VMEM((nq, rows, width), jnp.int32),
                pltpu.VMEM((rows, width), jnp.int32),
                pltpu.VMEM((nq, rows, width), F32),
                pltpu.VMEM((total, width), F32),
                pltpu.VMEM((n_tile, 24, width), F32),
                pltpu.VMEM((n_tile, 24, width), F32),
                pltpu.VMEM((nq, n_tile * CAP, 2 * width), BF16),
                dma((nk,)), dma((5,)), dma((2, nk)), dma((2, nk)), dma((2,)), dma((2,)),
                dma((n_chan - 1, nk)), dma((n_chan, nk)),
                dma((n_tile - 1,)), dma((n_tile,)),
            ],
            compiler_params=pltpu.CompilerParams(
                collective_id=0, has_side_effects=True, vmem_limit_bytes=49152 * 1024
            ),
        )(*[pltpu.with_memory_space_constraint(v, pltpu.HBM) for v in (intensity, block_pick, owner_tile, source_index, mask_low, mask_high)])
        return (
            maps.reshape(1, 1, n_tile, CAP, 8 * 128),
            spectra.reshape(1, 1, SRC_DEV, total),
            smoothed,
        )

    return jax.shard_map(
        step,
        mesh=mesh,
        in_specs=(
            P("chan", "tile", None),
            P("tile", "chan", None),
            P("tile", "chan", None),
            P("tile", "chan", None),
            P("tile", "chan", None, None),
            P("tile", "chan", None, None),
        ),
        out_specs=(
            P("tile", "chan", None, None, None),
            P("tile", "chan", None, None),
            P(None, "tile", "chan"),
        ),
        check_vma=False,
    )
```
